32 devices in a mesh: groups: 2 (over y), stretch: 4 (over z), fsdp: 2 (over x), head: 2 (over core).
Axes of the slice: x: 2, y: 2, z: 4, core: 2. Of those that a mesh axis runs over, the one named last changes fastest.
Arguments:
- hidden_in: bfloat16 [4096, 7168], P(('groups', 'stretch'), ('fsdp', 'head')), parts along dimension 0, may hold values from -6 to 6
- queries: bfloat16 [4096, 4096], P(('groups', 'stretch'), ('fsdp', 'head')), parts along dimension 0, may hold values from -110 to 110
- kv_weight: bfloat16 [7168, 2, 2, 512], P('fsdp', None, 'head'), may hold values from -0.0625 to 0.0625
- block_lists: int32 [32, 8], P(('groups', 'stretch')), parts along dimension 0, may hold values from 0 to 15, as said below
Outputs:
- attended: bfloat16 [4096, 4096], P(('groups', 'stretch'), ('fsdp', 'head')), parts along dimension 0
The draws below stay inside these ranges and needn't reach their ends.
There are 2 independent parts, one for each index of `groups`. The reference program is written for one: setup_inputs(seed, part) draws one part's arguments, and reference() takes and returns one part's arrays. A program takes and returns all parts, laid end to end along the dimension named above; an argument that names none is the same for every part. Nothing has to cross between parts.
Inputs may be any that keep to these rules, and one draw needn't show every extreme that they name: `block_lists`: query block i of span c = i // 4 names itself and max(i - 1, 4 * c); all query blocks of one span name the same blocks outside that span, which lie in earlier spans, at most one block of each earlier span; for c > 0 they include block 0 and a block of span c - 1; the first span names only its own blocks.
All inputs are finite; a program needn't handle non-finite values.
Results may differ from the reference program's by a relative error of at most 0.011.
Values may be sent and summed in bfloat16 or wider, within the bound.
A program may use at most 128 MiB of HBM per device.

```python
import math
import jax
import jax.numpy as jnp
from jax import lax

D = 7168
KVH = 8
GQ = 4
HD = 128
BLK = 128
KSEL = 8
TOK_DEV = 512
HQ = 32
KVD = 2
TOKENS = 2048
NB = 16
N_FSDP = 2
N_HEAD = 2


def draw_queries(key, part):
    key = jax.random.fold_in(key, 12)
    key_base = jax.random.fold_in(key, 0)
    values = jnp.clip(jax.random.normal(key_base, (TOKENS, HQ, HD), jnp.float32), -4.0, 4.0)
    return values.reshape(TOKENS, HQ * HD).astype(jnp.bfloat16)


def draw_block_lists(key, part):
    key = jax.random.fold_in(key, 11)
    key_offset, key_sender = jax.random.split(key, 2)
    per_span = TOK_DEV // BLK
    spans = TOKENS // TOK_DEV
    span_ids = jnp.arange(spans, dtype=jnp.int32)
    offsets = jax.random.randint(key_offset, (spans, spans), 0, per_span)
    offsets = jnp.where(span_ids[None, :] == 0, 0, offsets)
    senders = jax.random.randint(key_sender, (spans, KSEL - 4), 0, jnp.maximum(span_ids, 1)[:, None])
    fixed_senders = jnp.stack([jnp.maximum(span_ids - 1, 0), jnp.zeros_like(span_ids)], axis=1)
    all_senders = jnp.concatenate([fixed_senders, senders], axis=1)
    extra_blocks = all_senders * per_span + jnp.take_along_axis(offsets, all_senders, axis=1)
    block_ids = jnp.arange(NB, dtype=jnp.int32)
    owner = block_ids // per_span
    own_prev = jnp.maximum(block_ids - 1, owner * per_span)
    extras = jnp.take(extra_blocks, owner, axis=0)
    extras = jnp.where(owner[:, None] == 0, block_ids[:, None], extras)
    return jnp.concatenate([block_ids[:, None], own_prev[:, None], extras], axis=1).astype(jnp.int32)


def block_scale(rng, dims, shards, least, top_value):
    factor_of = 1.0
    for axis_at, shards_of in shards:
        heights = jax.random.uniform(jax.random.fold_in(jax.random.fold_in(rng, 6), axis_at), (shards_of,), jnp.float32, least / len(shards), top_value / len(shards))
        factor_of = factor_of * jnp.repeat(jnp.exp(heights), dims[axis_at] // shards_of).reshape((-1,) + (1,) * (len(dims) - 1 - axis_at))
    return factor_of


def scatter_about(stream_key, extent, scale, reach, cuts=(), held_as=jnp.bfloat16):
    factor_of = block_scale(stream_key, extent, cuts, -0.22, 0.18) if cuts else 1.0
    drawn = jax.random.normal(stream_key, extent, jnp.float32) * scale * factor_of
    return jnp.minimum(jnp.maximum(drawn, -reach), reach).astype(held_as)


def setup_inputs(seed: int = 0, part: int = 0) -> dict:
    streams_of = jax.random.split(jax.random.key(seed), 5)
    own_keys = jax.random.split(jax.random.fold_in(streams_of[4], part), 5)
    return {
        "hidden_in": scatter_about(own_keys[0], (TOKENS, D), 1.0, 6.0, ((0, 4), (1, 4))),
        "queries": draw_queries(jax.random.fold_in(jax.random.fold_in(streams_of[4], part), 71), part),
        "kv_weight": scatter_about(streams_of[2], (D, N_FSDP, N_HEAD, KVD * 2 * HD), D ** -0.5, 0.0625, ((0, 2), (2, 2))),
        "block_lists": draw_block_lists(jax.random.fold_in(jax.random.fold_in(streams_of[4], part), 71), part),
    }


THETA = 5000000.0


def rotate(keys, positions):
    width = keys.shape[-1]
    half = width // 2
    freq = jnp.exp(jnp.arange(half, dtype=jnp.float32) * (-2.0 * math.log(THETA) / width))
    angle = positions.astype(jnp.float32)[:, None, None] * freq
    cosine = jnp.cos(angle)
    sine = jnp.sin(angle)
    upper = keys[..., :half]
    lower = keys[..., half:]
    return jnp.concatenate([upper * cosine - lower * sine, lower * cosine + upper * sine], axis=-1)


def attend_block(items):
    query_blk, key_sel, value_sel, names, block_index = items
    block_size = query_blk.shape[0]
    count = names.shape[0]
    scale = query_blk.shape[-1] ** -0.5
    scores = jnp.einsum("qhgd,kthd->hgqkt", query_blk.astype(jnp.float32), key_sel.astype(jnp.float32)) * scale
    query_pos = block_index * block_size + jnp.arange(block_size, dtype=jnp.int32)
    key_pos = names[:, None] * block_size + jnp.arange(block_size, dtype=jnp.int32)[None, :]
    slot = jnp.arange(count, dtype=jnp.int32)
    earlier = (names[:, None] == names[None, :]) & (slot[None, :] < slot[:, None])
    first_seen = jnp.logical_not(jnp.any(earlier, axis=1))
    valid = (key_pos[None, :, :] <= query_pos[:, None, None]) & first_seen[None, :, None]
    scores = jnp.where(valid[None, None], scores, -jnp.inf)
    top = jnp.max(scores, axis=(3, 4), keepdims=True)
    weights = jnp.exp(scores - top)
    totals = jnp.sum(weights, axis=(3, 4))
    probs = weights.astype(jnp.bfloat16)
    mixed = jnp.einsum("hgqkt,kthd->qhgd", probs.astype(jnp.float32), value_sel.astype(jnp.float32))
    return (mixed / jnp.transpose(totals, (2, 0, 1))[..., None]).astype(jnp.bfloat16)


def reference(hidden_in, queries, kv_weight, block_lists):
    projected = jnp.dot(hidden_in, kv_weight.reshape(D, -1), preferred_element_type=jnp.float32)
    projected = projected.reshape(TOKENS, KVH, 2, HD)
    positions = jnp.arange(TOKENS, dtype=jnp.int32)
    keys = rotate(projected[:, :, 0], positions).astype(jnp.bfloat16)
    values = projected[:, :, 1].astype(jnp.bfloat16)
    key_blocks = keys.reshape(NB, BLK, KVH, HD)
    value_blocks = values.reshape(NB, BLK, KVH, HD)
    grouped = queries.reshape(NB, BLK, KVH, GQ, HD)

    def one_block(items):
        query_blk, names, block_index = items
        key_sel = jnp.take(key_blocks, names, axis=0)
        value_sel = jnp.take(value_blocks, names, axis=0)
        return attend_block((query_blk, key_sel, value_sel, names, block_index))

    result = lax.map(one_block, (grouped, block_lists, jnp.arange(NB, dtype=jnp.int32)))
    return result.reshape(TOKENS, HQ * HD)
```

```python
import functools
import math

import jax
import jax.numpy as jnp
from jax import lax
from jax.experimental import pallas as pl
from jax.experimental.pallas import tpu as pltpu
from jax.sharding import PartitionSpec as P

GQ = 4
HD = 128
BLK = 128
THETA = 5000000.0
MESH = pl.DeviceIdType.MESH
FAR = -1e30


def kernel(
    S, F, H,
    hidden_hbm, queries_hbm, weight_hbm, lists_hbm, lists_smem,
    out_hbm,
    hid, raw, weight, own, part_send, part_recv, kv, selected, slots,
    lists_in, lists_far, q, acc, top, total, out,
    load_sems, weight_sems, hid_send, hid_recv, part_send_sems, part_recv_sems,
    lists_send, lists_recv, lists_copy, slot_send, slot_recv, out_sems,
):
    s = lax.axis_index("stretch")
    f = lax.axis_index("fsdp")
    h = lax.axis_index("head")
    rows, quarter = hidden_hbm.shape
    cols = weight_hbm.shape[2]
    kv_local = cols // (2 * HD)
    heads = kv_local * GQ
    nb = rows // BLK
    factor = math.log2(math.e) * HD ** -0.5

    own_hidden = pltpu.make_async_copy(hidden_hbm, hid.at[h], load_sems.at[0])
    own_hidden.start()
    weight_loads = []
    for i in range(H):
        load = pltpu.make_async_copy(
            weight_hbm.at[pl.ds(i * quarter, quarter)],
            raw.at[pl.ds(i * quarter, quarter)],
            weight_sems.at[i],
        )
        load.start()
        weight_loads.append(load)
    load_q = pltpu.make_async_copy(queries_hbm, q, load_sems.at[1])
    load_q.start()

    barrier = pltpu.get_barrier_semaphore()
    for axis, here, size in (("head", h, H), ("fsdp", f, F), ("stretch", s, S)):
        for d in range(1, size):
            pl.semaphore_signal(
                barrier, inc=1, device_id={axis: lax.rem(here + d, size)}, device_id_type=MESH
            )
    pl.semaphore_wait(barrier, (H - 1) + (F - 1) + (S - 1))

    def hidden_copy(d, b, slot):
        r = pl.ds(b * BLK, BLK)
        return pltpu.make_async_remote_copy(
            src_ref=hidden_hbm.at[r],
            dst_ref=hid.at[slot, r],
            send_sem=hid_send.at[d - 1, b],
            recv_sem=hid_recv.at[d - 1, b],
            device_id={"head": lax.rem(h + d, H)},
            device_id_type=MESH,
        )

    for b in range(nb):
        for d in range(1, H):
            hidden_copy(d, b, h).start()

    def lists_copy_to(d):
        return pltpu.make_async_remote_copy(
            src_ref=lists_hbm,
            dst_ref=lists_in.at[d - 1],
            send_sem=lists_send.at[d - 1],
            recv_sem=lists_recv.at[d - 1],
            device_id={"stretch": lax.rem(s + S - d, S)},
            device_id_type=MESH,
        )

    for d in range(1, S):
        @pl.when(s >= d)
        def _(d=d):
            lists_copy_to(d).start()

    for i in range(H):
        weight_loads[i].wait()

        @pl.loop(0, quarter // BLK)
        def _(t, i=i):
            k0 = pl.multiple_of(i * quarter + t * BLK, BLK)
            for g in range(F):
                weight[g, pl.ds(k0, BLK)] = raw[pl.ds(k0, BLK), g, :]

    own_hidden.wait()

    def part_copy(d, b):
        r = pl.ds(b * BLK, BLK)
        return pltpu.make_async_remote_copy(
            src_ref=part_send.at[d - 1, r],
            dst_ref=part_recv.at[d - 1, r],
            send_sem=part_send_sems.at[d - 1, b],
            recv_sem=part_recv_sems.at[d - 1, b],
            device_id={"fsdp": lax.rem(f + d, F)},
            device_id_type=MESH,
        )

    def partial(r, target):
        result = None
        for i in range(H):
            term = jnp.dot(
                hid[i, r], weight[target, pl.ds(i * quarter, quarter)],
                preferred_element_type=jnp.float32,
            )
            result = term if result is None else result + term
        return result

    for b in range(nb):
        r = pl.ds(b * BLK, BLK)
        for d in range(1, H):
            hidden_copy(d, b, lax.rem(h + H - d, H)).wait_recv()
        for d in range(1, F):
            part_send[d - 1, r] = partial(r, lax.rem(f + d, F)).astype(jnp.bfloat16)
            part_copy(d, b).start()

    half_rows = 2 * BLK

    @pl.loop(0, rows // half_rows)
    def _(t):
        r = pl.ds(pl.multiple_of(t * half_rows, half_rows), half_rows)
        own[r] = partial(r, f)

    lane = lax.broadcasted_iota(jnp.int32, (1, HD), 1)
    lane_half = lax.rem(lane, HD // 2).astype(jnp.float32)
    freq = jnp.exp(lane_half * (-2.0 * math.log(THETA) / HD))
    sign = jnp.where(lane < HD // 2, -1.0, 1.0).astype(jnp.float32)
    for b in range(nb):
        r = pl.ds(b * BLK, BLK)
        position = s * rows + b * BLK + lax.broadcasted_iota(jnp.int32, (BLK, 1), 0)
        angle = position.astype(jnp.float32) * freq
        cosine = jnp.cos(angle)
        sine = jnp.sin(angle) * sign
        for d in range(1, F):
            part_copy(d, b).wait_recv()
        whole = own[r]
        for d in range(1, F):
            whole = whole + part_recv[d - 1, r].astype(jnp.float32)
        for j in range(kv_local):
            key = whole[:, 2 * j * HD : (2 * j + 1) * HD]
            swapped = jnp.concatenate([key[:, HD // 2 :], key[:, : HD // 2]], axis=1)
            kv[r, 2 * j * HD : (2 * j + 1) * HD] = (key * cosine + swapped * sine).astype(jnp.bfloat16)
            kv[r, (2 * j + 1) * HD : (2 * j + 2) * HD] = whole[
                :, (2 * j + 1) * HD : (2 * j + 2) * HD
            ].astype(jnp.bfloat16)

    def slot_copy(d):
        return pltpu.make_async_remote_copy(
            src_ref=selected.at[d - 1],
            dst_ref=slots.at[d - 1],
            send_sem=slot_send.at[d - 1],
            recv_sem=slot_recv.at[d - 1],
            device_id={"stretch": lax.rem(s + d, S)},
            device_id_type=MESH,
        )

    for d in range(1, S):
        @pl.when(s + d < S)
        def _(d=d):
            lists_copy_to(d).wait_recv()
            to_smem = pltpu.make_async_copy(lists_in.at[d - 1], lists_far.at[d - 1], lists_copy.at[d - 1])
            to_smem.start()
            to_smem.wait()
            block = jnp.int32(0)
            for n in range(lists_smem.shape[1]):
                name = lists_far[d - 1, 0, n]
                block = jnp.where((name >= s * nb) & (name < (s + 1) * nb), name - s * nb, block)
            chosen = None
            for b in range(nb):
                hot = jnp.where(block == b, 1.0, 0.0).astype(jnp.float32)
                term = kv[pl.ds(b * BLK, BLK)].astype(jnp.float32) * hot
                chosen = term if chosen is None else chosen + term
            selected[d - 1] = chosen.astype(jnp.bfloat16)
            slot_copy(d).start()

    load_q.wait()
    names = [[lists_smem[i, n] for n in range(lists_smem.shape[1])] for i in range(nb)]

    def named(i, block):
        found = names[i][0] == block
        for n in range(1, len(names[i])):
            found = found | (names[i][n] == block)
        return found

    biases = [
        [jnp.where(named(i, s * nb + j), 0.0, FAR).astype(jnp.float32) for j in range(i)]
        for i in range(nb)
    ]
    triangle = lax.broadcasted_iota(jnp.int32, (BLK, BLK), 0) >= lax.broadcasted_iota(
        jnp.int32, (BLK, BLK), 1
    )
    NT = (((1,), (1,)), ((), ()))

    @pl.loop(0, heads)
    def _(hd):
        lanes = pl.ds(pl.multiple_of(hd * HD, HD), HD)
        base = (hd // GQ) * (2 * HD)
        key_lanes = pl.ds(pl.multiple_of(base, HD), HD)
        value_lanes = pl.ds(pl.multiple_of(base + HD, HD), HD)
        for i in range(nb):
            r = pl.ds(i * BLK, BLK)
            n = (i + 1) * BLK
            scores = lax.dot_general(
                q[r, lanes], kv[pl.ds(0, n), key_lanes], NT, preferred_element_type=jnp.float32
            )
            pieces = [scores[:, j * BLK : (j + 1) * BLK] + biases[i][j] for j in range(i)]
            pieces.append(jnp.where(triangle, scores[:, i * BLK :], FAR))
            scores = jnp.concatenate(pieces, axis=1) if i else pieces[0]
            high = jnp.max(scores, axis=1, keepdims=True)
            weights = jnp.exp2((scores - high) * factor)
            top[hd, r] = jnp.broadcast_to(high, (BLK, HD))
            total[hd, r] = jnp.broadcast_to(jnp.sum(weights, axis=1, keepdims=True), (BLK, HD))
            acc[hd, r] = jnp.dot(
                weights.astype(jnp.bfloat16), kv[pl.ds(0, n), value_lanes],
                preferred_element_type=jnp.float32,
            )

    for d in range(1, S):
        @pl.when(s >= d)
        def _(d=d):
            slot_copy(d).wait_recv()
            low = (s - d) * nb
            found = (names[0][0] >= low) & (names[0][0] < low + nb)
            for n in range(1, len(names[0])):
                found = found | ((names[0][n] >= low) & (names[0][n] < low + nb))
            bias = jnp.where(found, 0.0, FAR).astype(jnp.float32)

            @pl.loop(0, heads)
            def _(hd):
                lanes = pl.ds(pl.multiple_of(hd * HD, HD), HD)
                base = (hd // GQ) * (2 * HD)
                keys = slots[d - 1, :, pl.ds(pl.multiple_of(base, HD), HD)]
                values = slots[d - 1, :, pl.ds(pl.multiple_of(base + HD, HD), HD)]
                for t in range(rows // half_rows):
                    r = pl.ds(t * half_rows, half_rows)
                    scores = lax.dot_general(
                        q[r, lanes], keys, NT, preferred_element_type=jnp.float32
                    ) + bias
                    before = top[hd, r]
                    high = jnp.maximum(before, jnp.max(scores, axis=1, keepdims=True))
                    weights = jnp.exp2((scores - high) * factor)
                    decay = jnp.exp2((before - high) * factor)
                    top[hd, r] = high
                    total[hd, r] = total[hd, r] * decay + jnp.sum(weights, axis=1, keepdims=True)
                    acc[hd, r] = acc[hd, r] * decay + jnp.dot(
                        weights.astype(jnp.bfloat16), values, preferred_element_type=jnp.float32
                    )

    @pl.loop(0, heads)
    def _(hd):
        lanes = pl.ds(pl.multiple_of(hd * HD, HD), HD)
        out[:, lanes] = (acc[hd] / total[hd]).astype(jnp.bfloat16)

    store = pltpu.make_async_copy(out, out_hbm, out_sems.at[0])
    store.start()

    for b in range(nb):
        for d in range(1, H):
            hidden_copy(d, b, h).wait_send()
        for d in range(1, F):
            part_copy(d, b).wait_send()
    for d in range(1, S):
        @pl.when(s >= d)
        def _(d=d):
            lists_copy_to(d).wait_send()

        @pl.when(s + d < S)
        def _(d=d):
            slot_copy(d).wait_send()
    store.wait()


def per_device(S, F, H, hidden_in, queries, kv_weight, block_lists):
    rows, quarter = hidden_in.shape
    depth, _, _, cols = kv_weight.shape
    heads = cols // (2 * HD) * GQ
    nb = rows // BLK
    bf16 = jnp.bfloat16
    dma = pltpu.SemaphoreType.DMA
    spans = max(S - 1, 1)
    return pl.pallas_call(
        functools.partial(kernel, S, F, H),
        out_shape=jax.ShapeDtypeStruct(queries.shape, bf16),
        in_specs=[pl.BlockSpec(memory_space=pl.ANY)] * 4 + [pl.BlockSpec(memory_space=pltpu.SMEM)],
        out_specs=pl.BlockSpec(memory_space=pl.ANY),
        scratch_shapes=[
            pltpu.VMEM((H, rows, quarter), bf16),
            pltpu.VMEM((depth, F, cols), bf16),
            pltpu.VMEM((F, depth, cols), bf16),
            pltpu.VMEM((rows, cols), jnp.float32),
            pltpu.VMEM((F - 1, rows, cols), bf16),
            pltpu.VMEM((F - 1, rows, cols), bf16),
            pltpu.VMEM((rows, cols), bf16),
            pltpu.VMEM((spans, BLK, cols), bf16),
            pltpu.VMEM((spans, BLK, cols), bf16),
            pltpu.VMEM((spans,) + block_lists.shape, jnp.int32),
            pltpu.SMEM((spans,) + block_lists.shape, jnp.int32),
            pltpu.VMEM(queries.shape, bf16),
            pltpu.VMEM((heads, rows, HD), jnp.float32),
            pltpu.VMEM((heads, rows, HD), jnp.float32),
            pltpu.VMEM((heads, rows, HD), jnp.float32),
            pltpu.VMEM(queries.shape, bf16),
            dma((2,)),
            dma((H,)),
            dma((H - 1, nb)),
            dma((H - 1, nb)),
            dma((F - 1, nb)),
            dma((F - 1, nb)),
            dma((spans,)),
            dma((spans,)),
            dma((spans,)),
            dma((spans,)),
            dma((spans,)),
            dma((1,)),
        ],
        compiler_params=pltpu.CompilerParams(
            collective_id=0, has_side_effects=True, vmem_limit_bytes=56 * 2**20
        ),
        cost_estimate=pl.CostEstimate(flops=6 * 10**9, bytes_accessed=12 * 2**20, transcendentals=3 * 10**6),
    )(
        hidden_in, queries, jnp.transpose(kv_weight, (0, 2, 1, 3)).reshape(depth, F, cols),
        block_lists, block_lists,
    )


def solution(mesh):
    in_specs = (
        P(("groups", "stretch"), ("fsdp", "head")),
        P(("groups", "stretch"), ("fsdp", "head")),
        P("fsdp", None, "head", None),
        P(("groups", "stretch"), None),
    )
    out_specs = P(("groups", "stretch"), ("fsdp", "head"))
    body = functools.partial(per_device, mesh.shape["stretch"], mesh.shape["fsdp"], mesh.shape["head"])
    return jax.shard_map(body, mesh=mesh, in_specs=in_specs, out_specs=out_specs, check_vma=False)
```

```python
import functools
import math

import jax
import jax.numpy as jnp
from jax import lax
from jax.experimental import pallas as pl
from jax.experimental.pallas import tpu as pltpu
from jax.sharding import PartitionSpec as P

GQ = 4
HD = 128
BLK = 128
THETA = 5000000.0
MESH = pl.DeviceIdType.MESH
FAR = -1e30
GROUP = 3
UNROLL = 7


def kernel(
    S, F, H,
    hidden_hbm, queries_hbm, weight_hbm, lists_hbm, lists_smem,
    out_hbm,
    hid, raw, weight, own, part_send, part_recv, kept, kv, selected, slots,
    cosines, sines, lists_in, lists_far, named, q, acc, top, out,
    load_sems, weight_sems, hid_send, hid_recv, part_send_sems, part_recv_sems,
    lists_send, lists_recv, lists_copy, slot_send, slot_recv, out_sems,
):
    s = lax.axis_index("stretch")
    f = lax.axis_index("fsdp")
    h = lax.axis_index("head")
    nb, _, quarter = hidden_hbm.shape
    rows = nb * BLK
    cols = weight_hbm.shape[2]
    kv_local = cols // (2 * HD)
    entries = lists_smem.shape[1]
    factor = math.log2(math.e) * HD ** -0.5
    NT = (((1,), (1,)), ((), ()))

    piece = quarter * F
    flat = weight_hbm.reshape(weight_hbm.shape[0] * F, cols)
    weight_loads = []
    for i in range(H):
        load = pltpu.make_async_copy(
            flat.at[pl.ds(i * piece, piece)], raw.at[pl.ds(i * piece, piece)], weight_sems.at[i]
        )
        load.start()
        weight_loads.append(load)
    own_hidden = pltpu.make_async_copy(hidden_hbm, hid.at[h], load_sems.at[0])
    own_hidden.start()
    load_q = pltpu.make_async_copy(queries_hbm, q, load_sems.at[1])
    load_q.start()

    barrier = pltpu.get_barrier_semaphore()
    for axis, here, size in (("head", h, H), ("fsdp", f, F), ("stretch", s, S)):
        for d in range(1, size):
            pl.semaphore_signal(
                barrier, inc=1, device_id={axis: lax.rem(here + d, size)}, device_id_type=MESH
            )
    pl.semaphore_wait(barrier, (H - 1) + (F - 1) + (S - 1))

    def lists_copy_to(d):
        return pltpu.make_async_remote_copy(
            src_ref=lists_hbm,
            dst_ref=lists_in.at[d - 1],
            send_sem=lists_send.at[d - 1],
            recv_sem=lists_recv.at[d - 1],
            device_id={"stretch": lax.rem(s + S - d, S)},
            device_id_type=MESH,
        )

    for d in range(1, S):
        @pl.when(s >= d)
        def _(d=d):
            lists_copy_to(d).start()

    def hidden_copy(d, slot):
        return pltpu.make_async_remote_copy(
            src_ref=hidden_hbm,
            dst_ref=hid.at[slot],
            send_sem=hid_send.at[d - 1],
            recv_sem=hid_recv.at[d - 1],
            device_id={"head": lax.rem(h + d, H)},
            device_id_type=MESH,
        )

    for d in range(1, H):
        hidden_copy(d, h).start()

    step = 2 * BLK
    each = step // F
    to = lax.broadcasted_iota(jnp.int32, (step, step), 0)
    at = lax.broadcasted_iota(jnp.int32, (step, step), 1)
    permute = jnp.where(lax.rem(to, each) * F + to // each == at, 1.0, 0.0).astype(jnp.bfloat16)
    for i in range(H):
        weight_loads[i].wait()

        @pl.loop(0, piece // step, unroll=UNROLL)
        def _(t, i=i):
            n0 = pl.multiple_of(i * piece + t * step, step)
            k0 = pl.multiple_of(i * quarter + t * each, each)
            sorted_rows = jnp.dot(
                permute, raw[pl.ds(n0, step)], preferred_element_type=jnp.float32
            ).astype(jnp.bfloat16)
            for g in range(F):
                weight[g, pl.ds(k0, each)] = sorted_rows[g * each : (g + 1) * each]

    for d in range(1, S):
        named[d - 1] = -1

        @pl.when(s + d < S)
        def _(d=d):
            lists_copy_to(d).wait_recv()
            to_smem = pltpu.make_async_copy(
                lists_in.at[d - 1], lists_far.at[d - 1], lists_copy.at[d - 1]
            )
            to_smem.start()
            to_smem.wait()
            block = jnp.int32(-1)
            for n in range(entries):
                name = lists_far[d - 1, 0, n]
                block = jnp.where((name >= s * nb) & (name < (s + 1) * nb), name - s * nb, block)
            named[d - 1] = block

    rank = []
    for b in range(nb):
        value = jnp.int32(S + b)
        for d in range(S - 1, 0, -1):
            value = jnp.where(named[d - 1] == b, d, value)
        rank.append(value)
    place = []
    for b in range(nb):
        value = jnp.int32(0)
        for other in range(nb):
            if other != b:
                value = value + jnp.where(rank[other] < rank[b], 1, 0)
        place.append(value)
    order = []
    for p in range(nb):
        value = jnp.int32(0)
        for b in range(1, nb):
            value = jnp.where(place[b] == p, b, value)
        order.append(value)

    def part_copy(d, p):
        return pltpu.make_async_remote_copy(
            src_ref=part_send.at[d - 1, p],
            dst_ref=part_recv.at[d - 1, p],
            send_sem=part_send_sems.at[d - 1, p],
            recv_sem=part_recv_sems.at[d - 1, p],
            device_id={"fsdp": lax.rem(f + d, F)},
            device_id_type=MESH,
        )

    def partial(activations, target):
        result = None
        for i in range(H):
            term = jnp.dot(
                activations(i), weight[target, pl.ds(i * quarter, quarter)],
                preferred_element_type=jnp.float32,
            )
            result = term if result is None else result + term
        return result

    own_hidden.wait()
    for d in range(1, H):
        hidden_copy(d, lax.rem(h + H - d, H)).wait_recv()
    for p in range(nb):
        for d in range(1, F):
            part_send[d - 1, p] = partial(
                lambda i: hid[i, order[p]], lax.rem(f + d, F)
            ).astype(jnp.bfloat16)
            part_copy(d, p).start()

    for t in range(nb // 2):
        both = partial(lambda i: hid[i, pl.ds(2 * t, 2)].reshape(2 * BLK, quarter), f)
        own[2 * t] = both[:BLK]
        own[2 * t + 1] = both[BLK:]

    lane = lax.broadcasted_iota(jnp.int32, (1, HD), 1)
    lane_half = lax.rem(lane, HD // 2).astype(jnp.float32)
    freq = jnp.exp(lane_half * (-2.0 * math.log(THETA) / HD))
    sign = jnp.where(lane < HD // 2, -1.0, 1.0).astype(jnp.float32)
    for b in range(nb):
        position = s * rows + b * BLK + lax.broadcasted_iota(jnp.int32, (BLK, 1), 0)
        angle = position.astype(jnp.float32) * freq
        cosines[b] = jnp.cos(angle)
        sines[b] = jnp.sin(angle) * sign

    def slot_copy(d):
        return pltpu.make_async_remote_copy(
            src_ref=selected.at[d - 1],
            dst_ref=slots.at[pl.ds((d - 1) * BLK, BLK)],
            send_sem=slot_send.at[d - 1],
            recv_sem=slot_recv.at[d - 1],
            device_id={"stretch": lax.rem(s + d, S)},
            device_id_type=MESH,
        )

    def send_named(d):
        spot = jnp.int32(0)
        for b in range(1, nb):
            spot = jnp.where(named[d - 1] == b, place[b], spot)
        spot = jnp.where(named[d - 1] == 0, place[0], spot)
        selected[d - 1] = kept[spot]
        slot_copy(d).start()

    for p in range(nb):
        for d in range(1, F):
            part_copy(d, p).wait_recv()
        whole = own[order[p]]
        for d in range(1, F):
            whole = whole + part_recv[d - 1, p].astype(jnp.float32)
        cosine = cosines[order[p]]
        sine = sines[order[p]]
        for j in range(kv_local):
            key = whole[:, 2 * j * HD : (2 * j + 1) * HD]
            swapped = jnp.concatenate([key[:, HD // 2 :], key[:, : HD // 2]], axis=1)
            kept[p, :, 2 * j * HD : (2 * j + 1) * HD] = (key * cosine + swapped * sine).astype(
                jnp.bfloat16
            )
            kept[p, :, (2 * j + 1) * HD : (2 * j + 2) * HD] = whole[
                :, (2 * j + 1) * HD : (2 * j + 2) * HD
            ].astype(jnp.bfloat16)
        for d in range(1, S):
            if p == 0:
                @pl.when((s == 0) & (s + d < S))
                def _(d=d):
                    send_named(d)
            if p == min(d, nb) - 1:
                @pl.when((s > 0) & (s + d < S))
                def _(d=d):
                    send_named(d)

    for b in range(nb):
        kv[pl.ds(b * BLK, BLK)] = kept[place[b]]

    load_q.wait()
    names = [[lists_smem[i, n] for n in range(entries)] for i in range(nb)]

    def lists_block(i, block):
        found = names[i][0] == block
        for n in range(1, entries):
            found = found | (names[i][n] == block)
        return found

    below = lax.broadcasted_iota(jnp.int32, (GQ * BLK, BLK), 1)
    triangle = lax.rem(lax.broadcasted_iota(jnp.int32, (GQ * BLK, BLK), 0), BLK) >= below

    def stacked_queries(j, i):
        return jnp.concatenate(
            [
                q[pl.ds(i * BLK, BLK), (j * GQ + g) * HD : (j * GQ + g + 1) * HD]
                for g in range(GQ)
            ],
            axis=0,
        )

    def with_ones(values):
        return jnp.concatenate([values, jnp.ones_like(values)], axis=1)

    for j in range(kv_local):
        key_lanes = slice(2 * j * HD, (2 * j + 1) * HD)
        value_lanes = slice((2 * j + 1) * HD, (2 * j + 2) * HD)
        for i in range(nb):
            n = (i + 1) * BLK
            scores = lax.dot_general(
                stacked_queries(j, i), kv[0:n, key_lanes], NT, preferred_element_type=jnp.float32
            )
            pieces = []
            for k in range(i):
                bias = jnp.where(lists_block(i, s * nb + k), 0.0, FAR).astype(jnp.float32)
                pieces.append(scores[:, k * BLK : (k + 1) * BLK] + bias)
            pieces.append(jnp.where(triangle, scores[:, i * BLK :], FAR))
            scores = jnp.concatenate(pieces, axis=1) if i else pieces[0]
            high = jnp.max(scores, axis=1, keepdims=True)
            weights = jnp.exp2((scores - high) * factor).astype(jnp.bfloat16)
            top[j, i] = jnp.broadcast_to(high, (GQ * BLK, HD))
            acc[j, i] = jnp.dot(
                weights, with_ones(kv[0:n, value_lanes]), preferred_element_type=jnp.float32
            )

    for d in range(1, S):
        @pl.when(s < d)
        def _(d=d):
            slots[pl.ds((d - 1) * BLK, BLK)] = jnp.zeros((BLK, cols), jnp.bfloat16)

    def store(i):
        r = pl.ds(i * BLK, BLK)
        return pltpu.make_async_copy(out.at[r], out_hbm.at[r], out_sems.at[i])

    def finish(j, i, mixed):
        result = mixed[:, :HD] / mixed[:, HD:]
        for g in range(GQ):
            out[pl.ds(i * BLK, BLK), (j * GQ + g) * HD : (j * GQ + g + 1) * HD] = result[
                g * BLK : (g + 1) * BLK
            ].astype(jnp.bfloat16)
        if j == kv_local - 1:
            store(i).start()

    last = max(range(1, S, GROUP), default=0)
    for first in range(1, S, GROUP):
        group = range(first, min(first + GROUP, S))

        @pl.when(s >= first)
        def _(first=first, group=group):
            biases = []
            for d in group:
                @pl.when(s >= d)
                def _(d=d):
                    slot_copy(d).wait_recv()
                low = (s - d) * nb
                found = (names[0][0] >= low) & (names[0][0] < low + nb)
                for n in range(1, entries):
                    found = found | ((names[0][n] >= low) & (names[0][n] < low + nb))
                biases.append(jnp.where(found & (s >= d), 0.0, FAR).astype(jnp.float32))
            held = pl.ds((first - 1) * BLK, len(group) * BLK)
            for i in range(nb):
                for j in range(kv_local):
                    keys = slots[held, 2 * j * HD : (2 * j + 1) * HD]
                    values = with_ones(slots[held, (2 * j + 1) * HD : (2 * j + 2) * HD])
                    scores = lax.dot_general(
                        stacked_queries(j, i), keys, NT, preferred_element_type=jnp.float32
                    )
                    scores = jnp.concatenate(
                        [scores[:, k * BLK : (k + 1) * BLK] + biases[k] for k in range(len(group))],
                        axis=1,
                    )
                    before = top[j, i]
                    high = jnp.maximum(before, jnp.max(scores, axis=1, keepdims=True))
                    weights = jnp.exp2((scores - high[:, :1]) * factor).astype(jnp.bfloat16)
                    decay = jnp.exp2((before - high) * factor)
                    mixed = acc[j, i] * jnp.concatenate([decay, decay], axis=1) + jnp.dot(
                        weights, values, preferred_element_type=jnp.float32
                    )
                    if first == last:
                        finish(j, i, mixed)
                    else:
                        top[j, i] = high
                        acc[j, i] = mixed

    @pl.when(s < max(last, 1))
    def _():
        for i in range(nb):
            for j in range(kv_local):
                finish(j, i, acc[j, i])

    for d in range(1, H):
        hidden_copy(d, h).wait_send()
    for p in range(nb):
        for d in range(1, F):
            part_copy(d, p).wait_send()
    for d in range(1, S):
        @pl.when(s >= d)
        def _(d=d):
            lists_copy_to(d).wait_send()

        @pl.when(s + d < S)
        def _(d=d):
            slot_copy(d).wait_send()
    for i in range(nb):
        store(i).wait()


def per_device(S, F, H, hidden_in, queries, kv_weight, block_lists):
    rows, quarter = hidden_in.shape
    depth, _, _, cols = kv_weight.shape
    kv_local = cols // (2 * HD)
    nb = rows // BLK
    bf16 = jnp.bfloat16
    f32 = jnp.float32
    dma = pltpu.SemaphoreType.DMA
    spans = max(S - 1, 1)
    return pl.pallas_call(
        functools.partial(kernel, S, F, H),
        out_shape=jax.ShapeDtypeStruct(queries.shape, bf16),
        in_specs=[pl.BlockSpec(memory_space=pl.ANY)] * 4 + [pl.BlockSpec(memory_space=pltpu.SMEM)],
        out_specs=pl.BlockSpec(memory_space=pl.ANY),
        scratch_shapes=[
            pltpu.VMEM((H, nb, BLK, quarter), bf16),
            pltpu.VMEM((depth * F, cols), bf16),
            pltpu.VMEM((F, depth, cols), bf16),
            pltpu.VMEM((nb, BLK, cols), f32),
            pltpu.VMEM((F - 1, nb, BLK, cols), bf16),
            pltpu.VMEM((F - 1, nb, BLK, cols), bf16),
            pltpu.VMEM((nb, BLK, cols), bf16),
            pltpu.VMEM((rows, cols), bf16),
            pltpu.VMEM((spans, BLK, cols), bf16),
            pltpu.VMEM((spans * BLK, cols), bf16),
            pltpu.VMEM((nb, BLK, HD), f32),
            pltpu.VMEM((nb, BLK, HD), f32),
            pltpu.VMEM((spans,) + block_lists.shape, jnp.int32),
            pltpu.SMEM((spans,) + block_lists.shape, jnp.int32),
            pltpu.SMEM((spans,), jnp.int32),
            pltpu.VMEM(queries.shape, bf16),
            pltpu.VMEM((kv_local, nb, GQ * BLK, 2 * HD), f32),
            pltpu.VMEM((kv_local, nb, GQ * BLK, HD), f32),
            pltpu.VMEM(queries.shape, bf16),
            dma((2,)),
            dma((H,)),
            dma((H - 1,)),
            dma((H - 1,)),
            dma((F - 1, nb)),
            dma((F - 1, nb)),
            dma((spans,)),
            dma((spans,)),
            dma((spans,)),
            dma((spans,)),
            dma((spans,)),
            dma((nb,)),
        ],
        compiler_params=pltpu.CompilerParams(
            collective_id=0, has_side_effects=True, vmem_limit_bytes=56 * 2**20
        ),
        cost_estimate=pl.CostEstimate(flops=6 * 10**9, bytes_accessed=12 * 2**20, transcendentals=3 * 10**6),
    )(
        hidden_in.reshape(nb, BLK, quarter), queries,
        jnp.transpose(kv_weight, (0, 2, 1, 3)).reshape(depth, F, cols),
        block_lists, block_lists,
    )


def solution(mesh):
    in_specs = (
        P(("groups", "stretch"), ("fsdp", "head")),
        P(("groups", "stretch"), ("fsdp", "head")),
        P("fsdp", None, "head", None),
        P(("groups", "stretch"), None),
    )
    out_specs = P(("groups", "stretch"), ("fsdp", "head"))
    body = functools.partial(per_device, mesh.shape["stretch"], mesh.shape["fsdp"], mesh.shape["head"])
    return jax.shard_map(body, mesh=mesh, in_specs=in_specs, out_specs=out_specs, check_vma=False)
```
